512 devices in a mesh: blk: 32 (over y, z_lo, core), grp: 16 (over z_hi, x).
Axes of the slice: x: 4, y: 8, z: 8 (z_hi: 4, z_lo: 2; z = z_hi * 2 + z_lo), core: 2. Of those that a mesh axis runs over, the one named last changes fastest.
Arguments:
- points: bfloat16 [16, 65536], P(None, ('blk', 'grp')), may hold values from -6 to 6, as said below
- right_side: float32 [64, 65536], P(None, ('blk', 'grp')), may hold values from -10 to 16
- nugget: float32 [65536], P(('blk', 'grp')), may hold values from 2 to 3
- scales: float32 [16], replicated, may hold values from 0.8 to 1.25
- pairs: int32 [32, 3], replicated, may hold values 0 or 1
Outputs:
- solution: float32 [64, 65536], P(None, ('blk', 'grp'))
- residual: float32 [64, 65536], P(None, ('blk', 'grp'))
The draws below stay inside these ranges and needn't reach their ends.
Inputs may be any that keep to these rules, and one draw needn't show every extreme that they name: pairs[b, d - 1] is 1 when block b and block (b + d) mod 32 share a tile. In features 0 and 1 the points of block b lie on the circle of radius 32 / (2 pi) about the anchor, at arc lengths from b to b + 3 + 1 (measured round the circle from feature 1 = 0), one point in each of 2048 equal slots of that arc; features 2 to 15 lie between 0 and 0.3.
All inputs are finite; a program needn't handle non-finite values.
Results may differ from the reference program's by a relative error of at most 0.0006.
Values may be sent and summed in bfloat16 or wider, within the bound.
A program may use at most 64 MiB of HBM per device.

```python
import math
import jax
import jax.numpy as jnp
from jax import lax

ROWS_DEV = 128
FEAT = 16
NRHS = 64
MAXP = 3
ITERS = 2
BLOCK = 2048
NBLOCKS = 32
POINTS = 65536
N_BLK = 32
N_GRP = 16


def layout(key):
    slot_keys = jax.random.split(jax.random.fold_in(key, 1), NBLOCKS)
    places = jax.vmap(lambda each_key: jax.random.permutation(each_key, BLOCK))(slot_keys).astype(jnp.float32)
    jitter = jax.random.uniform(jax.random.fold_in(key, 2), (NBLOCKS, BLOCK), jnp.float32)
    anchor = jnp.arange(NBLOCKS, dtype=jnp.float32)[:, None]
    arc_pos = anchor + (MAXP + 1) * (places + jitter) / BLOCK
    angles = 2.0 * math.pi / NBLOCKS * arc_pos
    return angles.reshape(POINTS)


def draw_points(key, part):
    angles = layout(jax.random.fold_in(key, 11))
    radius = NBLOCKS / (2.0 * math.pi)
    circle = jnp.stack([radius * jnp.cos(angles), radius * jnp.sin(angles)], axis=0)
    other_key = jax.random.fold_in(key, 12)
    others = 0.2 * jax.random.uniform(other_key, (FEAT - 2, POINTS), jnp.float32)
    return jnp.concatenate([circle, others], axis=0).astype(jnp.bfloat16)


def draw_right_side(key, part):
    angles = layout(jax.random.fold_in(key, 11))
    level_key = jax.random.fold_in(key, 31)
    wave_key = jax.random.fold_in(key, 32)
    phase_key = jax.random.fold_in(key, 33)
    harmonic_key = jax.random.fold_in(key, 34)
    noise_key = jax.random.fold_in(key, 35)
    block_rank = jnp.repeat(jnp.arange(NBLOCKS, dtype=jnp.float32), BLOCK) / (NBLOCKS - 1)
    harmonic = jax.random.randint(harmonic_key, (NRHS, 1), 1, 4).astype(jnp.float32)
    phases = jax.random.uniform(phase_key, (NRHS, 1), jnp.float32, 0.0, 2.0 * math.pi)
    amplitude = jax.random.uniform(wave_key, (NRHS, 1), jnp.float32, 0.3, 0.8)
    wave_part = amplitude * jnp.cos(harmonic * angles[None, :] + phases)
    levels = jax.random.uniform(level_key, (NRHS, 1), jnp.float32, 0.6, 1.2)
    noise_part = 0.6 * jax.random.truncated_normal(noise_key, -4.0, 4.0, (NRHS, POINTS), jnp.float32)
    envelope = 1.0 + 2.0 * block_rank
    return (envelope[None, :] * (levels + wave_part + noise_part)).astype(jnp.float32)


def set_ends(entries, rng, least, top_value):
    index_at = [jax.random.randint(jax.random.fold_in(rng, axis), (), 0, length) for axis, length in enumerate(entries.shape)]
    widest = entries.shape.index(max(entries.shape))
    beside = index_at[:widest] + [(index_at[widest] + 1) % entries.shape[widest]] + index_at[widest + 1:]
    return entries.at[tuple(index_at)].set(least).at[tuple(beside)].set(top_value)


def shard_levels(own_key, extent, cuts, low, top_value):
    def one(axis_at, parts):
        draws = jax.random.uniform(jax.random.fold_in(jax.random.fold_in(own_key, 6), axis_at), (parts,), jnp.float32, low / len(cuts), top_value / len(cuts))
        return jnp.repeat(jnp.exp(draws), extent[axis_at] // parts).reshape((-1,) + (1,) * (len(extent) - axis_at - 1))

    level = one(*cuts[0])
    for cut in cuts[1:]:
        level = level * one(*cut)
    return level


def setup_inputs(seed: int = 0) -> dict:
    streams_of = jax.random.split(jax.random.key(seed), 6)
    points = draw_points(jax.random.fold_in(streams_of[5], 71), 0)
    right_side = draw_right_side(jax.random.fold_in(streams_of[5], 71), 0)
    nugget = jnp.clip(jnp.exp(math.log(3.0) - 0.4054651 * jax.random.uniform(streams_of[2], (POINTS,), jnp.float32) ** shard_levels(streams_of[2], (POINTS,), ((0, 512),), -0.2, 0.2)), 2.0, 3.0)
    scales = jnp.clip(jnp.exp(jax.random.uniform(streams_of[3], (FEAT,), jnp.float32, math.log(0.8), math.log(1.25))), 0.8, 1.25)
    pairs = set_ends((jax.random.randint(streams_of[4], (NBLOCKS, MAXP), 0, 3) < 2).astype(jnp.int32), jax.random.fold_in(streams_of[4], 1), 0, 1)
    return {"points": points, "right_side": right_side, "nugget": nugget, "scales": scales, "pairs": pairs}


def kernel_tile(row_z, col_z):
    cross = jnp.dot(row_z.T, col_z, precision=lax.Precision.HIGHEST, preferred_element_type=jnp.float32)
    squared = lax.optimization_barrier(jnp.sum(row_z * row_z, axis=0))[:, None] + lax.optimization_barrier(jnp.sum(col_z * col_z, axis=0))[None, :] - 2.0 * cross
    distance = jnp.sqrt(jnp.maximum(squared, 0.0))
    spare = jnp.maximum(1.0 - distance, 0.0)
    return (spare ** 4 * (4.0 * distance + 1.0)).astype(jnp.bfloat16)

def reference(points, right_side, nugget, scales, pairs):
    block = ROWS_DEV * N_GRP
    nblocks = N_BLK
    amp = 1.0 / (block + 16)
    scaled = points.astype(jnp.float32) / scales[:, None]

    def operate(direction):
        rounded = direction.astype(jnp.bfloat16).astype(jnp.float32)

        def visit(acc, index):
            start = (index * block).astype(jnp.int32)
            row_z = lax.dynamic_slice_in_dim(scaled, start, block, 1)
            row_v = lax.dynamic_slice_in_dim(rounded, start, block, 1)
            for offset in range(MAXP + 1):
                other = ((index + offset) % nblocks * block).astype(jnp.int32)
                col_z = lax.dynamic_slice_in_dim(scaled, other, block, 1)
                col_v = lax.dynamic_slice_in_dim(rounded, other, block, 1)
                tile = kernel_tile(row_z, col_z).astype(jnp.float32)
                if offset == 0:
                    weight = jnp.float32(1.0)
                else:
                    weight = pairs[index, offset - 1].astype(jnp.float32)
                ahead = weight * jnp.dot(col_v, tile.T, preferred_element_type=jnp.float32)
                current = lax.dynamic_slice_in_dim(acc, start, block, 1)
                acc = lax.dynamic_update_slice_in_dim(acc, current + ahead, start, 1)
                if offset > 0:
                    behind = weight * jnp.dot(row_v, tile, preferred_element_type=jnp.float32)
                    current = lax.dynamic_slice_in_dim(acc, other, block, 1)
                    acc = lax.dynamic_update_slice_in_dim(acc, current + behind, other, 1)
            return (acc, None)
        empty = jnp.zeros(direction.shape, jnp.float32)
        acc, unused = lax.scan(visit, empty, jnp.arange(nblocks, dtype=jnp.int32))
        return nugget[None, :] * direction + amp * acc
    solution = jnp.zeros(right_side.shape, jnp.float32)
    residual = right_side
    direction = right_side
    norm_now = lax.optimization_barrier(jnp.sum(residual * residual, axis=1))
    for step in range(ITERS):
        image = operate(direction)
        alpha = norm_now / lax.optimization_barrier(jnp.sum(direction * image, axis=1))
        solution = solution + alpha[:, None] * direction
        residual = residual - alpha[:, None] * image
        if step + 1 < ITERS:
            norm_next = lax.optimization_barrier(jnp.sum(residual * residual, axis=1))
            direction = residual + (norm_next / norm_now)[:, None] * direction
            norm_now = norm_next
    return (solution, residual)
```

```python
import jax
import jax.numpy as jnp
from jax import lax
from jax.experimental import pallas as pl
from jax.experimental.pallas import tpu as pltpu
from jax.sharding import PartitionSpec as P

MESH = pl.DeviceIdType.MESH
F32 = jnp.float32
BF16 = jnp.bfloat16
STEP = 0.38
FAR = 64.0
PIECE = 128
NRHS = 64
FEAT = 16
AMP = 1.0 / 2064.0 / 256.0


def split3(value):
    first = value.astype(BF16).astype(F32)
    rest = value - first
    second = rest.astype(BF16).astype(F32)
    return first, second, rest - second


def kernel(
    points_ref, right_ref, nugget_ref, scales_ref, pairs_ref,
    x_ref, res_ref,
    col_pts, row_pts, right_v, nugget_v, scales_s, pairs_s, pen_s,
    inv_v, row_ops, col_ops, tiles,
    v1, v2, p_rows, out1, out2, sib1, sib2, got1, got2, sib_got1, sib_got2, ar,
    local_sem, pts_send, pts_recv, rpts_send, rpts_recv, v1_send, v1_recv, v2_send, v2_recv,
    pr_send, pr_recv, sib_send, sib_recv, rs_send, rs_recv, ar_send, ar_recv,
):
    blk, grp = lax.axis_index("blk"), lax.axis_index("grp")
    chip, core = blk // 2, blk % 2
    side = 1 - 2 * core
    zlow = chip % 2
    zhigh, xat = grp // 4, grp % 4

    def device(chip_at, core_at, zhigh_at, x_at):
        return (
            lax.rem(chip_at + 32, 16) * 2 + core_at,
            lax.rem(zhigh_at + 8, 4) * 4 + lax.rem(x_at + 8, 4),
        )

    col_to = [
        device(chip + dm, cc, zhigh, xat + dx)
        for dm, cc in ((0, core), (side, core), (-side, 1 - core), (-2 * side, 1 - core))
        for dx in range(4)
    ]
    col_from = [
        device(chip - dm, cc, zhigh, xat - dx)
        for dm, cc in ((0, core), (side, core), (side, 1 - core), (2 * side, 1 - core))
        for dx in range(4)
    ]
    row_to = [device(chip, cc, zhigh + k, xat) for cc in (core, 1 - core) for k in range(4)]
    sum_to = [device(chip, core, zhigh - k, xat) for k in range(4)]
    sibling = device(chip, 1 - core, zhigh, xat)
    y_line = [device(chip + 2 * k, core, zhigh, xat) for k in range(8)]
    z_line = [
        device(chip + dz * (1 - 2 * zlow), core, zhigh + k, xat) for dz in range(2) for k in range(4)
    ]
    x_line = [device(chip, cc, zhigh, xat + k) for cc in (core, 1 - core) for k in range(4)]

    greet = col_from[1:] + y_line[1:] + z_line[1:] + x_line[4:] + row_to[5:]
    barrier = pltpu.get_barrier_semaphore()
    for target in greet:
        pl.semaphore_signal(barrier, inc=1, device_id=target, device_id_type=MESH)

    loads = [
        pltpu.make_async_copy(points_ref, col_pts.at[0], local_sem.at[0]),
        pltpu.make_async_copy(right_ref, right_v, local_sem.at[1]),
        pltpu.make_async_copy(scales_ref, scales_s, local_sem.at[2]),
        pltpu.make_async_copy(pairs_ref, pairs_s, local_sem.at[3]),
        pltpu.make_async_copy(nugget_ref, nugget_v, local_sem.at[4]),
    ]
    for load in loads:
        load.start()

    def remote(src, dst, send, recv, target):
        return pltpu.make_async_remote_copy(
            src_ref=src, dst_ref=dst, send_sem=send, recv_sem=recv, device_id=target, device_id_type=MESH
        )

    def lanes(ref, index):
        return ref.at[:, pl.ds(index * PIECE, PIECE)]

    loads[0].wait()
    pl.semaphore_wait(barrier, len(greet))
    row_copies = [
        remote(col_pts.at[0], row_pts.at[k], rpts_send.at[k], rpts_recv.at[k], row_to[k]) for k in range(1, 8)
    ]
    col_copies = [
        remote(col_pts.at[0], col_pts.at[i], pts_send.at[i], pts_recv.at[i], col_to[i]) for i in range(1, 16)
    ]
    for copy in row_copies + col_copies:
        copy.start()
    row_pts[0] = col_pts[0]

    loads[1].wait()
    v1[:, 0:PIECE] = right_v[...].astype(BF16)
    v1_copies = [
        remote(lanes(v1, 0), lanes(v1, i), v1_send.at[i], v1_recv.at[i], col_to[i]) for i in range(1, 16)
    ]
    for copy in v1_copies:
        copy.start()

    for load in loads[2:]:
        load.wait()
    for f in range(FEAT):
        inv_v[f : f + 1, :] = jnp.full((1, PIECE), scales_s[f], F32)
    inv_v[...] = 1.0 / (inv_v[...] * inv_v[...])

    def away(low, offset):
        value = pairs_s[lax.rem(low + 32, 32), offset - 1]
        return (1 - value).astype(F32) * FAR

    first = core == 0
    pen_s[0] = 0.0
    pen_s[1] = away(jnp.where(first, blk - 2, blk), 2)
    pen_s[2] = away(jnp.where(first, blk - 1, blk), 1)
    pen_s[3] = away(jnp.where(first, blk - 3, blk), 3)
    pen_s[4] = away(jnp.where(first, blk, blk - 1), 1)
    pen_s[5] = away(jnp.where(first, blk - 2, blk - 1), 3)
    pen_s[6] = away(jnp.where(first, blk - 1, blk - 1), 2)
    pen_s[7] = FAR

    at_row = lax.broadcasted_iota(jnp.int32, (FEAT, PIECE), 0)

    def norm_rows(pts):
        norm = jnp.sum(pts * pts * (16.0 * inv_v[...]), axis=0, keepdims=True)
        return [jnp.broadcast_to(part, (FEAT, PIECE)) for part in split3(norm)]

    for k in range(8):
        if k:
            row_copies[k - 1].wait_recv()
        pts = row_pts[k].astype(F32)
        one, two, three = norm_rows(pts)
        own = at_row == (6 if k < 4 else 7)
        extra = jnp.where((at_row < 3) | own, 1.0, 0.0)
        extra = jnp.where(at_row == 3, one, extra)
        extra = jnp.where(at_row == 4, two, extra)
        extra = jnp.where(at_row == 5, three, extra)
        span = slice(k * PIECE, (k + 1) * PIECE)
        for part in range(3):
            row_ops[part * FEAT : (part + 1) * FEAT, span] = row_pts[k]
        row_ops[3 * FEAT :, span] = extra.astype(BF16)

    def column(i, chunks):
        @pl.when(i > 0)
        def _():
            remote(col_pts.at[0], col_pts.at[i], pts_send.at[i], pts_recv.at[i], sibling).wait_recv()

        pts = col_pts[i].astype(F32)
        scaled = split3(pts * (-32.0 * inv_v[...]))
        one, two, three = norm_rows(pts)
        extra = jnp.where(at_row == 0, one, 0.0)
        extra = jnp.where(at_row == 1, two, extra)
        extra = jnp.where(at_row == 2, three, extra)
        extra = jnp.where((at_row >= 3) & (at_row < 6), 1.0, extra)
        extra = jnp.where(at_row == 6, pen_s[i // 4], extra)
        extra = jnp.where(at_row == 7, pen_s[i // 4 + 4], extra)
        for part in range(3):
            col_ops[part * FEAT : (part + 1) * FEAT, :] = scaled[part].astype(BF16)
        col_ops[3 * FEAT :, :] = extra.astype(BF16)
        start = pl.multiple_of(i * PIECE, PIECE)
        ops = col_ops[...]
        for chunk in range(chunks):
            span = slice(chunk * 256, (chunk + 1) * 256)
            squared = lax.dot_general(
                ops, row_ops[:, span], (((0,), (0,)), ((), ())), preferred_element_type=F32
            )
            squared = jnp.maximum(squared, 1e-12)
            spare = jnp.maximum(4.0 - squared * lax.rsqrt(squared), 0.0)
            second = spare * spare
            tiles[pl.ds(start, PIECE), span] = (second * second * (5.0 - spare)).astype(BF16)

    def column_all(i, carry):
        column(i, 4)
        return carry

    def column_own(i, carry):
        column(i, 2)
        return carry

    lax.fori_loop(0, 12, column_all, 0)
    lax.fori_loop(12, 16, column_own, 0)

    def apply(vec, sib, sib_got, out, got, which):
        mixed = jnp.dot(vec[:, :1536], tiles[:1536, 512:], preferred_element_type=F32)
        for k in range(4):
            sib[k] = mixed[:, k * PIECE : (k + 1) * PIECE]
        swap = remote(sib, sib_got, sib_send.at[which], sib_recv.at[which], sibling)
        swap.start()
        total = jnp.dot(vec[...], tiles[:, :512], preferred_element_type=F32)
        for k in range(4):
            out[k] = total[:, k * PIECE : (k + 1) * PIECE]
        return swap

    def spread(swap, sib_got, out, got, which):
        swap.wait_recv()
        copies = []
        for k in (2, 1, 3):
            out[k] = out[k] + sib_got[k]
            copies.append(
                remote(out.at[k], got.at[k], rs_send.at[4 * which + k], rs_recv.at[4 * which + k], sum_to[k])
            )
            copies[-1].start()
        return copies

    def collect(copies, sib_got, out, got):
        mine = out[0] + sib_got[0]
        for copy in copies:
            copy.wait_recv()
        return mine + got[1] + got[2] + got[3]

    for copy in v1_copies:
        copy.wait_recv()
    swap1 = apply(v1, sib1, sib_got1, out1, got1, 0)
    sums1 = spread(swap1, sib_got1, out1, got1, 0)
    right = right_v[...]
    nugget = jnp.broadcast_to(nugget_v[...], (NRHS, PIECE))
    image = nugget * right + AMP * collect(sums1, sib_got1, out1, got1)
    step_to = right - STEP * image
    rounded = step_to.astype(BF16)
    v2[:, 0:PIECE] = rounded
    p_rows[:, 0:PIECE] = rounded
    v2_copies = [
        remote(lanes(v2, 0), lanes(v2, i), v2_send.at[i], v2_recv.at[i], col_to[i]) for i in range(1, 16)
    ]
    pr_copies = [
        remote(lanes(v2, 0), lanes(p_rows, k), pr_send.at[k], pr_recv.at[k], row_to[k]) for k in range(1, 8)
    ]
    for copy in v2_copies + pr_copies:
        copy.start()

    ones = jnp.ones((8, PIECE), F32)

    def across(values):
        return lax.dot_general(
            ones, values, (((1,), (1,)), ((), ())), precision=lax.Precision.HIGHEST, preferred_element_type=F32
        )

    sums_a = across(jnp.concatenate([right * right, right * image], axis=0))
    ar[0, 0:1, :] = sums_a[0:1]

    for copy in v2_copies:
        copy.wait_recv()
    swap2 = apply(v2, sib2, sib_got2, out2, got2, 1)
    for copy in pr_copies:
        copy.wait_recv()
    form = jnp.zeros((NRHS, PIECE), F32)
    for k in range(4):
        form = form + p_rows[:, k * PIECE : (k + 1) * PIECE].astype(F32) * out2[k]
        form = form + p_rows[:, (k + 4) * PIECE : (k + 5) * PIECE].astype(F32) * sib2[k]
    form = nugget * step_to * step_to + AMP * form
    sums_b = across(jnp.concatenate([step_to * step_to, form], axis=0))
    ar[0, 1:2, :] = sums_b[0:1]

    def share(stage, line):
        copies = [
            remote(
                ar.at[8 * stage], ar.at[8 * stage + k],
                ar_send.at[8 * stage + k], ar_recv.at[8 * stage + k], line[k],
            )
            for k in range(1, 8)
        ]
        for copy in copies:
            copy.start()
        return copies

    def gathered(stage, copies):
        for copy in copies:
            copy.wait_recv()
        total = ar[8 * stage]
        for k in range(1, 8):
            total = total + ar[8 * stage + k]
        return total

    shares_y = share(0, y_line)
    sums2 = spread(swap2, sib_got2, out2, got2, 1)
    ar[8] = gathered(0, shares_y)
    shares_x = share(1, x_line)
    ar[16] = gathered(1, shares_x)
    shares_z = share(2, z_line)
    second_image = nugget * step_to + AMP * collect(sums2, sib_got2, out2, got2)
    total = gathered(2, shares_z)

    top, low = total[0:1], total[1:2]
    rr, ru = top, pltpu.roll(top, 64, 1)
    pp, pw = low, pltpu.roll(low, 64, 1)
    alpha = rr / ru
    share_p = alpha / STEP
    share_r = 1.0 - share_p
    rp = rr - STEP * ru
    pu = (rp - pp) / STEP
    rr_next = share_r * share_r * rr + 2.0 * share_r * share_p * rp + share_p * share_p * pp
    dir_r = share_r + rr_next / rr
    bend = dir_r * dir_r * ru + 2.0 * dir_r * share_p * pu + share_p * share_p * pw
    alpha_next = rr_next / bend
    along = alpha_next * dir_r
    coefs = jnp.concatenate(
        [
            alpha + along,
            alpha_next * share_p,
            share_r - along / STEP,
            share_p + along / STEP,
            -alpha_next * share_p,
            jnp.zeros((3, PIECE), F32),
        ],
        axis=0,
    )
    columns = coefs.T[:NRHS]
    x_ref[...] = columns[:, 0:1] * right + columns[:, 1:2] * step_to
    res_ref[...] = columns[:, 2:3] * right + columns[:, 3:4] * step_to + columns[:, 4:5] * second_image

    for copy in (
        row_copies + col_copies + v1_copies + sums1 + v2_copies + pr_copies + sums2
        + [swap1, swap2] + shares_y + shares_x + shares_z
    ):
        copy.wait_send()


def on_device(points, right_side, nugget, scales, pairs):
    dma = pltpu.SemaphoreType.DMA
    any_space = pl.BlockSpec(memory_space=pl.ANY)
    vmem = pl.BlockSpec(memory_space=pltpu.VMEM)
    return pl.pallas_call(
        kernel,
        out_shape=(
            jax.ShapeDtypeStruct((NRHS, PIECE), F32),
            jax.ShapeDtypeStruct((NRHS, PIECE), F32),
        ),
        in_specs=[any_space] * 5,
        out_specs=(vmem, vmem),
        scratch_shapes=[
            pltpu.VMEM((16, FEAT, PIECE), BF16),
            pltpu.VMEM((8, FEAT, PIECE), BF16),
            pltpu.VMEM((NRHS, PIECE), F32),
            pltpu.VMEM((1, PIECE), F32),
            pltpu.SMEM((FEAT,), F32),
            pltpu.SMEM((32, 3), jnp.int32),
            pltpu.SMEM((8,), F32),
            pltpu.VMEM((FEAT, PIECE), F32),
            pltpu.VMEM((4 * FEAT, 8 * PIECE), BF16),
            pltpu.VMEM((4 * FEAT, PIECE), BF16),
            pltpu.VMEM((16 * PIECE, 8 * PIECE), BF16),
            pltpu.VMEM((NRHS, 16 * PIECE), BF16),
            pltpu.VMEM((NRHS, 16 * PIECE), BF16),
            pltpu.VMEM((NRHS, 8 * PIECE), BF16),
        ]
        + [pltpu.VMEM((4, NRHS, PIECE), F32)] * 8
        + [
            pltpu.VMEM((24, 2, PIECE), F32),
            dma((5,)),
            dma((16,)), dma((16,)), dma((8,)), dma((8,)),
            dma((16,)), dma((16,)), dma((16,)), dma((16,)),
            dma((8,)), dma((8,)),
            dma((2,)), dma((2,)), dma((8,)), dma((8,)), dma((24,)), dma((24,)),
        ],
        compiler_params=pltpu.CompilerParams(
            collective_id=0, has_side_effects=True, vmem_limit_bytes=40 * 2**20
        ),
    )(points, right_side, nugget.reshape(1, PIECE), scales, pairs)


def solution(mesh):
    placed = (P(None, ("blk", "grp")), P(None, ("blk", "grp")), P(("blk", "grp")), P(), P())
    return jax.shard_map(
        on_device,
        mesh=mesh,
        in_specs=placed,
        out_specs=(P(None, ("blk", "grp")), P(None, ("blk", "grp"))),
        check_vma=False,
    )
```

```python
import jax
import jax.numpy as jnp
from jax import lax
from jax.experimental import pallas as pl
from jax.experimental.pallas import tpu as pltpu
from jax.sharding import PartitionSpec as P

MESH = pl.DeviceIdType.MESH
F32 = jnp.float32
BF16 = jnp.bfloat16
STEP = 0.38
FAR = 64.0
PIECE = 128
NRHS = 64
FEAT = 16
AMP = 1.0 / 2064.0 / 256.0


def split3(value):
    first = value.astype(BF16).astype(F32)
    rest = value - first
    second = rest.astype(BF16).astype(F32)
    return first, second, rest - second


def kernel(
    points_ref, right_ref, nugget_ref, scales_ref, pairs_ref,
    out_ref,
    col_pts, row_pts, right_v, nugget_v, scales_s, pairs_s, pen_s,
    inv_v, row_ops, col_ops, tiles,
    v1, v2, p_rows, out1, out2, sib1, sib2, got1, got2, sib_got1, sib_got2, ar,
    local_sem, pts_send, pts_recv, rpts_send, rpts_recv, v1_send, v1_recv, v2_send, v2_recv,
    pr_send, pr_recv, sib_send, sib_recv, rs_send, rs_recv, ar_send, ar_recv,
):
    blk, grp = lax.axis_index("blk"), lax.axis_index("grp")
    chip, core = blk // 2, blk % 2
    side = 1 - 2 * core
    zlow = chip % 2
    zhigh, xat = grp // 4, grp % 4

    def device(chip_at, core_at, zhigh_at, x_at):
        return (
            lax.rem(chip_at + 32, 16) * 2 + core_at,
            lax.rem(zhigh_at + 8, 4) * 4 + lax.rem(x_at + 8, 4),
        )

    col_to = [
        device(chip + dm, cc, zhigh, xat + dx)
        for dm, cc in ((0, core), (side, core), (-side, 1 - core), (-2 * side, 1 - core))
        for dx in range(4)
    ]
    col_from = [
        device(chip - dm, cc, zhigh, xat - dx)
        for dm, cc in ((0, core), (side, core), (side, 1 - core), (2 * side, 1 - core))
        for dx in range(4)
    ]
    row_to = [device(chip, cc, zhigh + k, xat) for cc in (core, 1 - core) for k in range(4)]
    sum_to = [device(chip, core, zhigh - k, xat) for k in range(4)]
    sibling = device(chip, 1 - core, zhigh, xat)
    y_line = [
        device(chip + 2 * k, cc, zhigh, xat)
        for cc, k in [(core, 0)] + [(cc, k) for k in (4, 3, 5, 2, 6, 1, 7, 0) for cc in (1 - core, core)][:-1]
    ]
    plane = sorted(
        ((min(2 * dz, 8 - 2 * dz) + (low if dz < 3 else -low) + min(dx, 4 - dx), dz, low, dx)
         for dz in range(4) for low in range(2) for dx in range(4)),
        key=lambda place: -place[0],
    )
    plane = plane[-1:] + plane[:-1]
    plane_line = [
        device(chip + low * (1 - 2 * zlow), core, zhigh + dz, xat + dx) for _, dz, low, dx in plane
    ]

    far_y = [device(chip + 8, cc, zhigh, xat) for cc in (core, 1 - core)]
    greet = far_y + col_from[1:] + row_to[1:]
    barrier = pltpu.get_barrier_semaphore()
    for target in greet:
        pl.semaphore_signal(barrier, inc=1, device_id=target, device_id_type=MESH)

    loads = [
        pltpu.make_async_copy(points_ref, col_pts.at[0], local_sem.at[0]),
        pltpu.make_async_copy(right_ref, right_v, local_sem.at[1]),
        pltpu.make_async_copy(scales_ref, scales_s, local_sem.at[2]),
        pltpu.make_async_copy(pairs_ref, pairs_s, local_sem.at[3]),
        pltpu.make_async_copy(nugget_ref, nugget_v, local_sem.at[4]),
    ]
    for load in loads:
        load.start()

    def remote(src, dst, send, recv, target):
        return pltpu.make_async_remote_copy(
            src_ref=src, dst_ref=dst, send_sem=send, recv_sem=recv, device_id=target, device_id_type=MESH
        )

    def lanes(ref, index):
        return ref.at[:, pl.ds(index * PIECE, PIECE)]

    loads[0].wait()
    pl.semaphore_wait(barrier, len(greet))
    row_copies = [
        remote(col_pts.at[0], row_pts.at[k], rpts_send.at[k], rpts_recv.at[k], row_to[k]) for k in range(1, 8)
    ]
    col_copies = [
        remote(col_pts.at[0], col_pts.at[i], pts_send.at[i], pts_recv.at[i], col_to[i]) for i in range(1, 16)
    ]
    for copy in row_copies + col_copies:
        copy.start()
    row_pts[0] = col_pts[0]

    loads[1].wait()
    v1[:, 0:PIECE] = right_v[...].astype(BF16)
    v1_copies = [
        remote(lanes(v1, 0), lanes(v1, i), v1_send.at[i], v1_recv.at[i], col_to[i]) for i in range(1, 16)
    ]
    for copy in v1_copies:
        copy.start()

    for load in loads[2:]:
        load.wait()
    for f in range(FEAT):
        inv_v[f : f + 1, :] = jnp.full((1, PIECE), scales_s[f], F32)
    inv_v[...] = 1.0 / (inv_v[...] * inv_v[...])

    def away(low, offset):
        value = pairs_s[offset - 1, lax.rem(low + 32, 32)]
        return (1 - value).astype(F32) * FAR

    first = core == 0
    pen_s[0] = 0.0
    pen_s[1] = away(jnp.where(first, blk - 2, blk), 2)
    pen_s[2] = away(jnp.where(first, blk - 1, blk), 1)
    pen_s[3] = away(jnp.where(first, blk - 3, blk), 3)
    pen_s[4] = away(jnp.where(first, blk, blk - 1), 1)
    pen_s[5] = away(jnp.where(first, blk - 2, blk - 1), 3)
    pen_s[6] = away(jnp.where(first, blk - 1, blk - 1), 2)
    pen_s[7] = FAR

    at_row = lax.broadcasted_iota(jnp.int32, (FEAT, PIECE), 0)

    def norm_rows(pts):
        norm = jnp.sum(pts * pts * (16.0 * inv_v[...]), axis=0, keepdims=True)
        return [jnp.broadcast_to(part, (FEAT, PIECE)) for part in split3(norm)]

    for k in range(8):
        if k:
            row_copies[k - 1].wait_recv()
        pts = row_pts[k].astype(F32)
        one, two, three = norm_rows(pts)
        own = at_row == (6 if k < 4 else 7)
        extra = jnp.where((at_row < 3) | own, 1.0, 0.0)
        extra = jnp.where(at_row == 3, one, extra)
        extra = jnp.where(at_row == 4, two, extra)
        extra = jnp.where(at_row == 5, three, extra)
        span = slice(k * PIECE, (k + 1) * PIECE)
        for part in range(3):
            row_ops[part * FEAT : (part + 1) * FEAT, span] = row_pts[k]
        row_ops[3 * FEAT :, span] = extra.astype(BF16)

    def columns_of(j, chunks):
        for part_at in range(4):
            i = j * 4 + part_at

            def arrived():
                remote(col_pts.at[0], col_pts.at[i], pts_send.at[i], pts_recv.at[i], sibling).wait_recv()

            if part_at == 0:
                pl.when(i > 0)(arrived)
            else:
                arrived()
            pts = col_pts[i].astype(F32)
            scaled = split3(pts * (-32.0 * inv_v[...]))
            one, two, three = norm_rows(pts)
            extra = jnp.where(at_row == 0, one, 0.0)
            extra = jnp.where(at_row == 1, two, extra)
            extra = jnp.where(at_row == 2, three, extra)
            extra = jnp.where((at_row >= 3) & (at_row < 6), 1.0, extra)
            extra = jnp.where(at_row == 6, pen_s[j], extra)
            extra = jnp.where(at_row == 7, pen_s[j + 4], extra)
            at = slice(part_at * PIECE, (part_at + 1) * PIECE)
            for part in range(3):
                col_ops[part * FEAT : (part + 1) * FEAT, at] = scaled[part].astype(BF16)
            col_ops[3 * FEAT :, at] = extra.astype(BF16)
        start = pl.multiple_of(j * 4 * PIECE, 4 * PIECE)
        ops = col_ops[...]
        for chunk in range(chunks):
            span = slice(chunk * 256, (chunk + 1) * 256)
            squared = lax.dot_general(
                ops, row_ops[:, span], (((0,), (0,)), ((), ())), preferred_element_type=F32
            )
            squared = jnp.maximum(squared, 1e-12)
            spare = jnp.maximum(4.0 - squared * lax.rsqrt(squared), 0.0)
            second = spare * spare
            tiles[pl.ds(start, 4 * PIECE), span] = (second * second * (5.0 - spare)).astype(BF16)

    def columns_all(j, carry):
        columns_of(j, 4)
        return carry

    lax.fori_loop(0, 3, columns_all, 0)
    columns_of(3, 2)

    def apply(vec, sib, sib_got, out, which, between):
        mixed = jnp.dot(vec[:, :1536], tiles[:1536, 512:], preferred_element_type=F32)
        for k in range(4):
            sib[k] = mixed[:, k * PIECE : (k + 1) * PIECE]
        swap = remote(sib, sib_got, sib_send.at[which], sib_recv.at[which], sibling)
        swap.start()
        between()
        total = jnp.dot(vec[...], tiles[:, :512], preferred_element_type=F32)
        for k in range(4):
            out[k] = total[:, k * PIECE : (k + 1) * PIECE]
        return swap

    def spread(swap, sib_got, out, got, which):
        swap.wait_recv()
        copies = []
        for k in (2, 1, 3):
            out[k] = out[k] + sib_got[k]
            copies.append(
                remote(out.at[k], got.at[k], rs_send.at[4 * which + k], rs_recv.at[4 * which + k], sum_to[k])
            )
            copies[-1].start()
        return copies

    def collect(copies, sib_got, out, got):
        mine = out[0] + sib_got[0]
        for copy in copies:
            copy.wait_recv()
        return mine + got[1] + got[2] + got[3]

    for copy in v1_copies:
        copy.wait_recv()
    swap1 = apply(v1, sib1, sib_got1, out1, 0, lambda: None)
    sums1 = spread(swap1, sib_got1, out1, got1, 0)
    right = right_v[...]
    nugget = jnp.broadcast_to(nugget_v[...], (NRHS, PIECE))
    image = nugget * right + AMP * collect(sums1, sib_got1, out1, got1)
    step_to = right - STEP * image
    rounded = step_to.astype(BF16)
    v2[:, 0:PIECE] = rounded
    p_rows[:, 0:PIECE] = rounded
    v2_copies = [
        remote(lanes(v2, 0), lanes(v2, i), v2_send.at[i], v2_recv.at[i], col_to[i]) for i in range(1, 16)
    ]
    pr_copies = [
        remote(lanes(v2, 0), lanes(p_rows, k), pr_send.at[k], pr_recv.at[k], row_to[k]) for k in range(1, 4)
    ]
    for copy in v2_copies + pr_copies:
        copy.start()
    hand_on = remote(
        p_rows.at[:, pl.ds(0, 4 * PIECE)], p_rows.at[:, pl.ds(4 * PIECE, 4 * PIECE)],
        pr_send.at[4], pr_recv.at[4], sibling,
    )

    def pass_rows():
        for copy in pr_copies:
            copy.wait_recv()
        hand_on.start()

    ones = jnp.ones((8, PIECE), F32)

    def across(values):
        return lax.dot_general(
            ones, values, (((1,), (1,)), ((), ())), precision=lax.Precision.HIGHEST, preferred_element_type=F32
        )

    sums_a = across(jnp.concatenate([right * right, right * image], axis=0))
    ar[0, 0:1, :] = sums_a[0:1]

    for copy in v2_copies:
        copy.wait_recv()
    swap2 = apply(v2, sib2, sib_got2, out2, 1, pass_rows)
    hand_on.wait_recv()
    form = jnp.zeros((NRHS, PIECE), F32)
    for k in range(4):
        form = form + p_rows[:, k * PIECE : (k + 1) * PIECE].astype(F32) * out2[k]
        form = form + p_rows[:, (k + 4) * PIECE : (k + 5) * PIECE].astype(F32) * sib2[k]
    form = nugget * step_to * step_to + AMP * form
    sums_b = across(jnp.concatenate([step_to * step_to, form], axis=0))
    ar[0, 1:2, :] = sums_b[0:1]

    def share(base, line):
        copies = [
            remote(
                ar.at[base], ar.at[base + k], ar_send.at[base + k], ar_recv.at[base + k], line[k],
            )
            for k in range(1, len(line))
        ]
        for copy in copies:
            copy.start()
        return copies

    def gathered(base, copies):
        for copy in copies:
            copy.wait_recv()
        terms = [ar[base + k] for k in range(len(copies) + 1)]
        while len(terms) > 1:
            terms = [a + b for a, b in zip(terms[::2], terms[1::2])]
        return terms[0]

    shares_y = share(0, y_line)
    sums2 = spread(swap2, sib_got2, out2, got2, 1)
    ar[16] = gathered(0, shares_y)
    shares_plane = share(16, plane_line)
    second_image = nugget * step_to + AMP * collect(sums2, sib_got2, out2, got2)
    total = gathered(16, shares_plane)

    top, low = total[0:1], total[1:2]
    rr, ru = top, pltpu.roll(top, 64, 1)
    pp, pw = low, pltpu.roll(low, 64, 1)
    alpha = rr / ru
    share_p = alpha / STEP
    share_r = 1.0 - share_p
    rp = rr - STEP * ru
    pu = (rp - pp) / STEP
    rr_next = share_r * share_r * rr + 2.0 * share_r * share_p * rp + share_p * share_p * pp
    dir_r = share_r + rr_next / rr
    bend = dir_r * dir_r * ru + 2.0 * dir_r * share_p * pu + share_p * share_p * pw
    alpha_next = rr_next / bend
    along = alpha_next * dir_r
    coefs = jnp.concatenate(
        [
            alpha + along,
            alpha_next * share_p,
            share_r - along / STEP,
            share_p + along / STEP,
            -alpha_next * share_p,
            jnp.zeros((3, PIECE), F32),
        ],
        axis=0,
    )
    columns = coefs.T[:NRHS]
    out_ref[:NRHS] = columns[:, 0:1] * right + columns[:, 1:2] * step_to
    out_ref[NRHS:] = columns[:, 2:3] * right + columns[:, 3:4] * step_to + columns[:, 4:5] * second_image

    for copy in (
        row_copies + col_copies + v1_copies + sums1 + v2_copies + pr_copies + sums2
        + [swap1, swap2, hand_on] + shares_y + shares_plane
    ):
        copy.wait_send()


def on_device(points, right_side, nugget, scales, pairs):
    dma = pltpu.SemaphoreType.DMA
    far_space = pl.BlockSpec(memory_space=pltpu.HBM)
    both = pl.pallas_call(
        kernel,
        out_shape=jax.ShapeDtypeStruct((2 * NRHS, PIECE), F32),
        in_specs=[far_space] * 5,
        out_specs=pl.BlockSpec(memory_space=pltpu.VMEM),
        scratch_shapes=[
            pltpu.VMEM((16, FEAT, PIECE), BF16),
            pltpu.VMEM((8, FEAT, PIECE), BF16),
            pltpu.VMEM((NRHS, PIECE), F32),
            pltpu.VMEM((1, PIECE), F32),
            pltpu.SMEM((FEAT,), F32),
            pltpu.SMEM((3, 32), jnp.int32),
            pltpu.SMEM((8,), F32),
            pltpu.VMEM((FEAT, PIECE), F32),
            pltpu.VMEM((4 * FEAT, 8 * PIECE), BF16),
            pltpu.VMEM((4 * FEAT, 4 * PIECE), BF16),
            pltpu.VMEM((16 * PIECE, 8 * PIECE), BF16),
            pltpu.VMEM((NRHS, 16 * PIECE), BF16),
            pltpu.VMEM((NRHS, 16 * PIECE), BF16),
            pltpu.VMEM((NRHS, 8 * PIECE), BF16),
        ]
        + [pltpu.VMEM((4, NRHS, PIECE), F32)] * 8
        + [
            pltpu.VMEM((48, 2, PIECE), F32),
            dma((5,)),
            dma((16,)), dma((16,)), dma((8,)), dma((8,)),
            dma((16,)), dma((16,)), dma((16,)), dma((16,)),
            dma((8,)), dma((8,)),
            dma((2,)), dma((2,)), dma((8,)), dma((8,)), dma((48,)), dma((48,)),
        ],
        compiler_params=pltpu.CompilerParams(
            collective_id=0, has_side_effects=True, vmem_limit_bytes=62 * 2**20
        ),
    )(points, right_side, nugget.reshape(1, PIECE), scales, pairs.T)
    return both[:NRHS], both[NRHS:]


def solution(mesh):
    placed = (P(None, ("blk", "grp")), P(None, ("blk", "grp")), P(("blk", "grp")), P(), P())
    return jax.shard_map(
        on_device,
        mesh=mesh,
        in_specs=placed,
        out_specs=(P(None, ("blk", "grp")), P(None, ("blk", "grp"))),
        check_vma=False,
    )
```

```python
import jax
import jax.numpy as jnp
from jax import lax
from jax.experimental import pallas as pl
from jax.experimental.pallas import tpu as pltpu
from jax.sharding import PartitionSpec as P

MESH = pl.DeviceIdType.MESH
F32 = jnp.float32
BF16 = jnp.bfloat16
STEP = 0.38
FAR = 64.0
PIECE = 128
NRHS = 64
FEAT = 16
AMP = 1.0 / 2064.0 / 256.0
SHIFTS = (0, 1, 3, 2)
GROUP = 4 * PIECE
SIB_GROUP = 3 * PIECE
FAR_FIRST = [4 * g + j for g in (3, 2, 1, 0) for j in (2, 1, 3, 0)][:-1]


def split3(value):
    first = value.astype(BF16).astype(F32)
    rest = value - first
    second = rest.astype(BF16).astype(F32)
    return first, second, rest - second


def kernel(
    points_ref, right_ref, nugget_ref, scales_ref, pairs_ref,
    out_ref,
    col_pts, row_pts, right_v, nugget_v, scales_s, pairs_s, pen_s,
    inv_v, row_ops, col_ops, tiles,
    v1, v2, p_rows, out1, out2, sib1, sib2, got1, got2, sib_got1, sib_got2, ar,
    local_sem, pts_send, pts_recv, rpts_send, rpts_recv, v1_send, v1_recv, v2_send, v2_recv,
    pr_send, pr_recv, sib_send, sib_recv, rs_send, rs_recv, ar_send, ar_recv,
):
    blk, grp = lax.axis_index("blk"), lax.axis_index("grp")
    chip, core = blk // 2, blk % 2
    side = 1 - 2 * core
    zlow = chip % 2
    zhigh, xat = grp // 4, grp % 4

    def device(chip_at, core_at, zhigh_at, x_at):
        return (
            lax.rem(chip_at + 32, 16) * 2 + core_at,
            lax.rem(zhigh_at + 8, 4) * 4 + lax.rem(x_at + 8, 4),
        )

    col_to = [
        device(chip + dm, cc, zhigh, xat + dx)
        for dx in SHIFTS
        for dm, cc in ((0, core), (side, core), (-side, 1 - core), (-2 * side, 1 - core))
    ]
    col_from = [
        device(chip - dm, cc, zhigh, xat - dx)
        for dx in SHIFTS
        for dm, cc in ((0, core), (side, core), (side, 1 - core), (2 * side, 1 - core))
    ]
    row_to = [device(chip, cc, zhigh + k, xat) for cc in (core, 1 - core) for k in range(4)]
    sum_to = [device(chip, core, zhigh - k, xat) for k in range(4)]
    sibling = device(chip, 1 - core, zhigh, xat)
    y_line = [
        device(chip + 2 * k, cc, zhigh, xat)
        for cc, k in [(core, 0)] + [(cc, k) for k in (4, 3, 5, 2, 6, 1, 7, 0) for cc in (1 - core, core)][:-1]
    ]
    plane = sorted(
        ((min(2 * dz, 8 - 2 * dz) + (low if dz < 3 else -low) + min(dx, 4 - dx), dz, low, dx)
         for dz in range(4) for low in range(2) for dx in range(4)),
        key=lambda place: -place[0],
    )
    plane = plane[-1:] + plane[:-1]
    plane_line = [
        device(chip + low * (1 - 2 * zlow), core, zhigh + dz, xat + dx) for _, dz, low, dx in plane
    ]

    far_y = [device(chip + 8, cc, zhigh, xat) for cc in (core, 1 - core)]
    greet = [col_from[i] for i in FAR_FIRST] + [row_to[k] for k in (2, 6, 1, 3, 5, 7, 4)] + far_y
    barrier = pltpu.get_barrier_semaphore()
    for target in greet:
        pl.semaphore_signal(barrier, inc=1, device_id=target, device_id_type=MESH)

    loads = [
        pltpu.make_async_copy(points_ref, col_pts.at[0], local_sem.at[0]),
        pltpu.make_async_copy(right_ref, right_v, local_sem.at[1]),
        pltpu.make_async_copy(scales_ref, scales_s, local_sem.at[2]),
        pltpu.make_async_copy(pairs_ref, pairs_s, local_sem.at[3]),
        pltpu.make_async_copy(nugget_ref, nugget_v, local_sem.at[4]),
    ]
    for load in loads:
        load.start()

    def remote(src, dst, send, recv, target):
        return pltpu.make_async_remote_copy(
            src_ref=src, dst_ref=dst, send_sem=send, recv_sem=recv, device_id=target, device_id_type=MESH
        )

    def lanes(ref, index):
        return ref.at[:, pl.ds(index * PIECE, PIECE)]

    loads[0].wait()
    pl.semaphore_wait(barrier, len(greet))
    row_copies = [
        remote(col_pts.at[0], row_pts.at[k], rpts_send.at[k], rpts_recv.at[k], row_to[k])
        for k in (2, 6, 1, 3, 5, 7, 4)
    ]
    col_copies = [
        remote(col_pts.at[0], col_pts.at[i], pts_send.at[i], pts_recv.at[i], col_to[i]) for i in FAR_FIRST
    ]
    for copy in row_copies + col_copies:
        copy.start()
    row_pts[0] = col_pts[0]

    loads[1].wait()
    v1[:, 0:PIECE] = right_v[...].astype(BF16)
    v1_copies = [
        remote(lanes(v1, 0), lanes(v1, i), v1_send.at[i], v1_recv.at[i], col_to[i]) for i in FAR_FIRST
    ]
    for copy in v1_copies:
        copy.start()

    for load in loads[2:]:
        load.wait()
    for f in range(FEAT):
        inv_v[f : f + 1, :] = jnp.full((1, PIECE), scales_s[f], F32)
    inv_v[...] = 1.0 / (inv_v[...] * inv_v[...])

    def away(low, offset):
        value = pairs_s[offset - 1, lax.rem(low + 32, 32)]
        return (1 - value).astype(F32) * FAR

    first = core == 0
    pen_s[0] = 0.0
    pen_s[1] = away(jnp.where(first, blk - 2, blk), 2)
    pen_s[2] = away(jnp.where(first, blk - 1, blk), 1)
    pen_s[3] = away(jnp.where(first, blk - 3, blk), 3)
    pen_s[4] = away(jnp.where(first, blk, blk - 1), 1)
    pen_s[5] = away(jnp.where(first, blk - 2, blk - 1), 3)
    pen_s[6] = away(jnp.where(first, blk - 1, blk - 1), 2)
    pen_s[7] = FAR

    at_row = lax.broadcasted_iota(jnp.int32, (FEAT, PIECE), 0)

    def norm_rows(pts):
        norm = jnp.sum(pts * pts * (16.0 * inv_v[...]), axis=0, keepdims=True)
        return [jnp.broadcast_to(part, (FEAT, PIECE)) for part in split3(norm)]

    for k in range(8):
        if k:
            remote(col_pts.at[0], row_pts.at[k], rpts_send.at[k], rpts_recv.at[k], sibling).wait_recv()
        pts = row_pts[k].astype(F32)
        one, two, three = norm_rows(pts)
        own = at_row == (6 if k < 4 else 7)
        extra = jnp.where((at_row < 3) | own, 1.0, 0.0)
        extra = jnp.where(at_row == 3, one, extra)
        extra = jnp.where(at_row == 4, two, extra)
        extra = jnp.where(at_row == 5, three, extra)
        span = slice(k * PIECE, (k + 1) * PIECE)
        for part in range(3):
            row_ops[part * FEAT : (part + 1) * FEAT, span] = row_pts[k]
        row_ops[3 * FEAT :, span] = extra.astype(BF16)

    def prepare(g):
        for j in range(4):
            i = g * 4 + j

            def arrived():
                remote(col_pts.at[0], col_pts.at[i], pts_send.at[i], pts_recv.at[i], sibling).wait_recv()

            if j == 0:
                pl.when(i > 0)(arrived)
            else:
                arrived()
            pts = col_pts[i].astype(F32)
            scaled = split3(pts * (-32.0 * inv_v[...]))
            one, two, three = norm_rows(pts)
            extra = jnp.where(at_row == 0, one, 0.0)
            extra = jnp.where(at_row == 1, two, extra)
            extra = jnp.where(at_row == 2, three, extra)
            extra = jnp.where((at_row >= 3) & (at_row < 6), 1.0, extra)
            extra = jnp.where(at_row == 6, pen_s[j], extra)
            extra = jnp.where(at_row == 7, pen_s[j + 4], extra)
            at = pl.ds(pl.multiple_of(i * PIECE, PIECE), PIECE)
            for part in range(3):
                col_ops[part * FEAT : (part + 1) * FEAT, at] = scaled[part].astype(BF16)
            col_ops[3 * FEAT :, at] = extra.astype(BF16)

    def entries(g, depth, first_row):
        at = pl.ds(pl.multiple_of(g * GROUP, GROUP), depth)
        ops = col_ops[:, at]
        for chunk in range(2):
            span = slice(first_row + chunk * 256, first_row + (chunk + 1) * 256)
            squared = lax.dot_general(
                ops, row_ops[:, span], (((0,), (0,)), ((), ())), preferred_element_type=F32
            )
            squared = jnp.maximum(squared, 1e-12)
            spare = jnp.maximum(4.0 - squared * lax.rsqrt(squared), 0.0)
            second = spare * spare
            tiles[at, span] = (second * second * (5.0 - spare)).astype(BF16)

    def near_group(g, carry):
        prepare(g)
        entries(g, SIB_GROUP, 512)
        entries(g, GROUP, 0)
        return carry

    def far_group(g, carry):
        prepare(g)
        entries(g, SIB_GROUP, 512)
        return carry

    def far_group_own(g, carry):
        entries(g, GROUP, 0)
        return carry

    def sib_part(vec, g):
        return jnp.dot(
            vec[:, g * GROUP : g * GROUP + SIB_GROUP],
            tiles[g * GROUP : g * GROUP + SIB_GROUP, 512:],
            preferred_element_type=F32,
        )

    def pieces(ref, values, first):
        for k in range(values.shape[1] // PIECE):
            ref[first + k] = values[:, k * PIECE : (k + 1) * PIECE]

    def spread(sib_got, out, got, which, order):
        copies = []
        for k in order:
            out[k] = out[k] + sib_got[k]
            copies.append(
                remote(out.at[k], got.at[k], rs_send.at[4 * which + k], rs_recv.at[4 * which + k], sum_to[k])
            )
            copies[-1].start()
        return copies

    def collect(copies, sib_got, out, got):
        mine = out[0] + sib_got[0]
        for copy in copies:
            copy.wait_recv()
        return mine + got[1] + got[2] + got[3]

    swap1 = remote(sib1, sib_got1, sib_send.at[0], sib_recv.at[0], sibling)
    swap2 = remote(sib2, sib_got2, sib_send.at[1], sib_recv.at[1], sibling)

    lax.fori_loop(0, 2, near_group, 0)
    lax.fori_loop(2, 4, far_group, 0)
    for copy in v1_copies:
        copy.wait_recv()
    pieces(sib1, sib_part(v1, 0) + sib_part(v1, 1) + sib_part(v1, 2) + sib_part(v1, 3), 0)
    swap1.start()
    lax.fori_loop(2, 4, far_group_own, 0)
    pieces(out1, jnp.dot(v1[...], tiles[:, 256:512], preferred_element_type=F32), 2)
    swap1.wait_recv()
    sums1 = spread(sib_got1, out1, got1, 0, (2, 3))
    pieces(out1, jnp.dot(v1[...], tiles[:, :256], preferred_element_type=F32), 0)
    sums1 = sums1 + spread(sib_got1, out1, got1, 0, (1,))
    right = right_v[...]
    nugget = jnp.broadcast_to(nugget_v[...], (NRHS, PIECE))
    image = nugget * right + AMP * collect(sums1, sib_got1, out1, got1)
    step_to = right - STEP * image
    rounded = step_to.astype(BF16)
    v2[:, 0:PIECE] = rounded
    p_rows[:, 0:PIECE] = rounded
    v2_copies = [
        remote(lanes(v2, 0), lanes(v2, i), v2_send.at[i], v2_recv.at[i], col_to[i]) for i in FAR_FIRST
    ]
    pr_copies = [
        remote(lanes(v2, 0), lanes(p_rows, k), pr_send.at[k], pr_recv.at[k], row_to[k]) for k in (2, 1, 3)
    ]
    for copy in v2_copies + pr_copies:
        copy.start()
    hand_on = remote(
        p_rows.at[:, pl.ds(0, 4 * PIECE)], p_rows.at[:, pl.ds(4 * PIECE, 4 * PIECE)],
        pr_send.at[4], pr_recv.at[4], sibling,
    )

    ones = jnp.ones((8, PIECE), F32)

    def across(values):
        return lax.dot_general(
            ones, values, (((1,), (1,)), ((), ())), precision=lax.Precision.HIGHEST, preferred_element_type=F32
        )

    sums_a = across(jnp.concatenate([right * right, right * image], axis=0))
    ar[0, 0:1, :] = sums_a[0:1]

    mixed = jnp.zeros((NRHS, 4 * PIECE), F32)
    total = jnp.zeros((NRHS, 4 * PIECE), F32)
    for g in range(4):
        for copy, i in zip(v2_copies, FAR_FIRST):
            if i // 4 == g:
                copy.wait_recv()
        mixed = mixed + sib_part(v2, g)
        if g == 3:
            for copy in pr_copies:
                copy.wait_recv()
            hand_on.start()
        total = total + jnp.dot(
            v2[:, g * GROUP : (g + 1) * GROUP],
            tiles[g * GROUP : (g + 1) * GROUP, :512],
            preferred_element_type=F32,
        )
    pieces(sib2, mixed, 0)
    pieces(out2, total, 0)
    form = jnp.zeros((NRHS, PIECE), F32)
    for k in range(4):
        form = form + p_rows[:, k * PIECE : (k + 1) * PIECE].astype(F32) * out2[k]
    hand_on.wait_recv()
    for k in range(4):
        form = form + p_rows[:, (k + 4) * PIECE : (k + 5) * PIECE].astype(F32) * sib2[k]
    form = nugget * step_to * step_to + AMP * form
    sums_b = across(jnp.concatenate([step_to * step_to, form], axis=0))
    ar[0, 1:2, :] = sums_b[0:1]

    def share(base, line):
        copies = [
            remote(
                ar.at[base], ar.at[base + k], ar_send.at[base + k], ar_recv.at[base + k], line[k],
            )
            for k in range(1, len(line))
        ]
        for copy in copies:
            copy.start()
        return copies

    def gathered(base, copies):
        for copy in copies:
            copy.wait_recv()
        terms = [ar[base + k] for k in range(len(copies) + 1)]
        while len(terms) > 1:
            terms = [a + b for a, b in zip(terms[::2], terms[1::2])]
        return terms[0]

    shares_y = share(0, y_line)
    swap2.start()
    swap2.wait_recv()
    sums2 = spread(sib_got2, out2, got2, 1, (2, 1, 3))
    ar[16] = gathered(0, shares_y)
    shares_plane = share(16, plane_line)
    second_image = nugget * step_to + AMP * collect(sums2, sib_got2, out2, got2)
    total = gathered(16, shares_plane)

    top, low = total[0:1], total[1:2]
    rr, ru = top, pltpu.roll(top, 64, 1)
    pp, pw = low, pltpu.roll(low, 64, 1)
    alpha = rr / ru
    share_p = alpha / STEP
    share_r = 1.0 - share_p
    rp = rr - STEP * ru
    pu = (rp - pp) / STEP
    rr_next = share_r * share_r * rr + 2.0 * share_r * share_p * rp + share_p * share_p * pp
    dir_r = share_r + rr_next / rr
    bend = dir_r * dir_r * ru + 2.0 * dir_r * share_p * pu + share_p * share_p * pw
    alpha_next = rr_next / bend
    along = alpha_next * dir_r
    coefs = jnp.concatenate(
        [
            alpha + along,
            alpha_next * share_p,
            share_r - along / STEP,
            share_p + along / STEP,
            -alpha_next * share_p,
            jnp.zeros((3, PIECE), F32),
        ],
        axis=0,
    )
    columns = coefs.T[:NRHS]
    out_ref[:NRHS] = columns[:, 0:1] * right + columns[:, 1:2] * step_to
    out_ref[NRHS:] = columns[:, 2:3] * right + columns[:, 3:4] * step_to + columns[:, 4:5] * second_image

    for copy in (
        row_copies + col_copies + v1_copies + sums1 + v2_copies + pr_copies + sums2
        + [swap1, swap2, hand_on] + shares_y + shares_plane
    ):
        copy.wait_send()


def on_device(points, right_side, nugget, scales, pairs):
    dma = pltpu.SemaphoreType.DMA
    operands = (points, right_side, nugget.reshape(1, PIECE), scales, pairs.T)
    operands = [pltpu.with_memory_space_constraint(array, pltpu.HBM) for array in operands]
    far_space = pl.BlockSpec(memory_space=pltpu.HBM)
    both = pl.pallas_call(
        kernel,
        out_shape=jax.ShapeDtypeStruct((2 * NRHS, PIECE), F32),
        in_specs=[far_space] * 5,
        out_specs=pl.BlockSpec(memory_space=pltpu.VMEM),
        scratch_shapes=[
            pltpu.VMEM((16, FEAT, PIECE), BF16),
            pltpu.VMEM((8, FEAT, PIECE), BF16),
            pltpu.VMEM((NRHS, PIECE), F32),
            pltpu.VMEM((1, PIECE), F32),
            pltpu.SMEM((FEAT,), F32),
            pltpu.SMEM((3, 32), jnp.int32),
            pltpu.SMEM((8,), F32),
            pltpu.VMEM((FEAT, PIECE), F32),
            pltpu.VMEM((4 * FEAT, 8 * PIECE), BF16),
            pltpu.VMEM((4 * FEAT, 16 * PIECE), BF16),
            pltpu.VMEM((16 * PIECE, 8 * PIECE), BF16),
            pltpu.VMEM((NRHS, 16 * PIECE), BF16),
            pltpu.VMEM((NRHS, 16 * PIECE), BF16),
            pltpu.VMEM((NRHS, 8 * PIECE), BF16),
        ]
        + [pltpu.VMEM((4, NRHS, PIECE), F32)] * 8
        + [
            pltpu.VMEM((48, 2, PIECE), F32),
            dma((5,)),
            dma((16,)), dma((16,)), dma((8,)), dma((8,)),
            dma((16,)), dma((16,)), dma((16,)), dma((16,)),
            dma((8,)), dma((8,)),
            dma((2,)), dma((2,)), dma((8,)), dma((8,)), dma((48,)), dma((48,)),
        ],
        compiler_params=pltpu.CompilerParams(
            collective_id=0, has_side_effects=True, vmem_limit_bytes=40 * 2**20
        ),
    )(*operands)
    return both[:NRHS], both[NRHS:]


def solution(mesh):
    placed = (P(None, ("blk", "grp")), P(None, ("blk", "grp")), P(("blk", "grp")), P(), P())
    return jax.shard_map(
        on_device,
        mesh=mesh,
        in_specs=placed,
        out_specs=(P(None, ("blk", "grp")), P(None, ("blk", "grp"))),
        check_vma=False,
    )
```

```python
import jax
import jax.numpy as jnp
from jax import lax
from jax.experimental import pallas as pl
from jax.experimental.pallas import tpu as pltpu
from jax.sharding import PartitionSpec as P

MESH = pl.DeviceIdType.MESH
F32 = jnp.float32
BF16 = jnp.bfloat16
STEP = 0.38
FAR = 64.0
PIECE = 128
NRHS = 64
FEAT = 16
AMP = 1.0 / 2064.0 / 256.0
SHIFTS = (0, 1, 3, 2)
GROUP = 4 * PIECE
SIB_GROUP = 3 * PIECE
FAR_FIRST = [4 * g + j for g in (3, 2, 1, 0) for j in (2, 1, 3, 0)][:-1]


def split3(value):
    first = value.astype(BF16).astype(F32)
    rest = value - first
    second = rest.astype(BF16).astype(F32)
    return first, second, rest - second


def kernel(
    points_ref, right_ref, nugget_ref, scales_ref, pairs_ref,
    out_ref,
    col_pts, row_pts, right_v, nugget_v, scales_s, pairs_s, pen_s,
    inv_v, row_ops, col_ops, tiles,
    v1, v2, v1_slots, v2_slots, p_rows, out1, out2, sib1, sib2, got1, got2, sib_got1, sib_got2, ar,
    local_sem, pts_send, pts_recv, rpts_send, rpts_recv, v1_send, v1_recv, v2_send, v2_recv,
    pr_send, pr_recv, sib_send, sib_recv, rs_send, rs_recv, ar_send, ar_recv,
):
    blk, grp = lax.axis_index("blk"), lax.axis_index("grp")
    chip, core = blk // 2, blk % 2
    side = 1 - 2 * core
    zlow = chip % 2
    zhigh, xat = grp // 4, grp % 4

    def device(chip_at, core_at, zhigh_at, x_at):
        return (
            lax.rem(chip_at + 32, 16) * 2 + core_at,
            lax.rem(zhigh_at + 8, 4) * 4 + lax.rem(x_at + 8, 4),
        )

    col_to = [
        device(chip + dm, cc, zhigh, xat + dx)
        for dx in SHIFTS
        for dm, cc in ((0, core), (side, core), (-side, 1 - core), (-2 * side, 1 - core))
    ]
    col_from = [
        device(chip - dm, cc, zhigh, xat - dx)
        for dx in SHIFTS
        for dm, cc in ((0, core), (side, core), (side, 1 - core), (2 * side, 1 - core))
    ]
    row_to = [device(chip, cc, zhigh + k, xat) for cc in (core, 1 - core) for k in range(4)]
    sum_to = [device(chip, core, zhigh - k, xat) for k in range(4)]
    sibling = device(chip, 1 - core, zhigh, xat)
    y_line = [
        device(chip + 2 * k, cc, zhigh, xat)
        for cc, k in [(core, 0)] + [(cc, k) for k in (4, 3, 5, 2, 6, 1, 7, 0) for cc in (1 - core, core)][:-1]
    ]
    plane = sorted(
        ((min(2 * dz, 8 - 2 * dz) + (low if dz < 3 else -low) + min(dx, 4 - dx), dz, low, dx)
         for dz in range(4) for low in range(2) for dx in range(4)),
        key=lambda place: -place[0],
    )
    plane = plane[-1:] + plane[:-1]
    plane_line = [
        device(chip + low * (1 - 2 * zlow), core, zhigh + dz, xat + dx) for _, dz, low, dx in plane
    ]

    far_y = [device(chip + 8, cc, zhigh, xat) for cc in (core, 1 - core)]
    greet = [col_from[i] for i in FAR_FIRST] + [row_to[k] for k in (2, 6, 1, 3, 5, 7, 4)] + far_y
    barrier = pltpu.get_barrier_semaphore()
    for target in greet:
        pl.semaphore_signal(barrier, inc=1, device_id=target, device_id_type=MESH)

    loads = [
        pltpu.make_async_copy(points_ref, col_pts.at[0], local_sem.at[0]),
        pltpu.make_async_copy(right_ref, right_v, local_sem.at[1]),
        pltpu.make_async_copy(scales_ref, scales_s, local_sem.at[2]),
        pltpu.make_async_copy(pairs_ref, pairs_s, local_sem.at[3]),
        pltpu.make_async_copy(nugget_ref, nugget_v, local_sem.at[4]),
    ]
    for load in loads:
        load.start()

    def remote(src, dst, send, recv, target):
        return pltpu.make_async_remote_copy(
            src_ref=src, dst_ref=dst, send_sem=send, recv_sem=recv, device_id=target, device_id_type=MESH
        )

    def lay_out(vec, slots, first, last):
        for i in range(first, last):
            vec[:, i * PIECE : (i + 1) * PIECE] = slots[i]

    loads[0].wait()
    pl.semaphore_wait(barrier, len(greet))
    row_copies = [
        remote(col_pts.at[0], row_pts.at[k], rpts_send.at[k], rpts_recv.at[k], row_to[k])
        for k in (2, 6, 1, 3, 5, 7, 4)
    ]
    col_copies = [
        remote(col_pts.at[0], col_pts.at[i], pts_send.at[i], pts_recv.at[i], col_to[i]) for i in FAR_FIRST
    ]
    for copy in row_copies + col_copies:
        copy.start()
    row_pts[0] = col_pts[0]

    loads[1].wait()
    v1_slots[0] = right_v[...].astype(BF16)
    v1_copies = [
        remote(v1_slots.at[0], v1_slots.at[i], v1_send.at[i], v1_recv.at[i], col_to[i]) for i in FAR_FIRST
    ]
    for copy in v1_copies:
        copy.start()

    for load in loads[2:]:
        load.wait()
    for f in range(FEAT):
        inv_v[f : f + 1, :] = jnp.full((1, PIECE), scales_s[f], F32)
    inv_v[...] = 1.0 / (inv_v[...] * inv_v[...])

    def away(low, offset):
        value = pairs_s[offset - 1, lax.rem(low + 32, 32)]
        return (1 - value).astype(F32) * FAR

    first = core == 0
    pen_s[0] = 0.0
    pen_s[1] = away(jnp.where(first, blk - 2, blk), 2)
    pen_s[2] = away(jnp.where(first, blk - 1, blk), 1)
    pen_s[3] = away(jnp.where(first, blk - 3, blk), 3)
    pen_s[4] = away(jnp.where(first, blk, blk - 1), 1)
    pen_s[5] = away(jnp.where(first, blk - 2, blk - 1), 3)
    pen_s[6] = away(jnp.where(first, blk - 1, blk - 1), 2)
    pen_s[7] = FAR

    at_row = lax.broadcasted_iota(jnp.int32, (FEAT, PIECE), 0)

    def norm_rows(pts):
        norm = jnp.sum(pts * pts * (16.0 * inv_v[...]), axis=0, keepdims=True)
        return [jnp.broadcast_to(part, (FEAT, PIECE)) for part in split3(norm)]

    for k in range(8):
        if k:
            remote(col_pts.at[0], row_pts.at[k], rpts_send.at[k], rpts_recv.at[k], sibling).wait_recv()
        pts = row_pts[k].astype(F32)
        one, two, three = norm_rows(pts)
        own = at_row == (6 if k < 4 else 7)
        extra = jnp.where((at_row < 3) | own, 1.0, 0.0)
        extra = jnp.where(at_row == 3, one, extra)
        extra = jnp.where(at_row == 4, two, extra)
        extra = jnp.where(at_row == 5, three, extra)
        span = slice(k * PIECE, (k + 1) * PIECE)
        for part in range(3):
            row_ops[part * FEAT : (part + 1) * FEAT, span] = row_pts[k]
        row_ops[3 * FEAT :, span] = extra.astype(BF16)

    def prepare(g):
        for j in range(4):
            i = g * 4 + j

            def arrived():
                remote(col_pts.at[0], col_pts.at[i], pts_send.at[i], pts_recv.at[i], sibling).wait_recv()

            if j == 0:
                pl.when(i > 0)(arrived)
            else:
                arrived()
            pts = col_pts[i].astype(F32)
            scaled = split3(pts * (-32.0 * inv_v[...]))
            one, two, three = norm_rows(pts)
            extra = jnp.where(at_row == 0, one, 0.0)
            extra = jnp.where(at_row == 1, two, extra)
            extra = jnp.where(at_row == 2, three, extra)
            extra = jnp.where((at_row >= 3) & (at_row < 6), 1.0, extra)
            extra = jnp.where(at_row == 6, pen_s[j], extra)
            extra = jnp.where(at_row == 7, pen_s[j + 4], extra)
            at = pl.ds(pl.multiple_of(i * PIECE, PIECE), PIECE)
            for part in range(3):
                col_ops[part * FEAT : (part + 1) * FEAT, at] = scaled[part].astype(BF16)
            col_ops[3 * FEAT :, at] = extra.astype(BF16)

    def entries(start, depth, first_row):
        at = pl.ds(start, depth)
        span = slice(first_row, first_row + 256)
        squared = lax.dot_general(
            col_ops[:, at], row_ops[:, span], (((0,), (0,)), ((), ())), preferred_element_type=F32
        )
        squared = jnp.maximum(squared, 1e-12)
        spare = jnp.maximum(4.0 - squared * lax.rsqrt(squared), 0.0)
        second = spare * spare
        tiles[at, span] = (second * second * (5.0 - spare)).astype(BF16)

    def sib_group(g, carry):
        prepare(g)
        start = pl.multiple_of(g * GROUP, GROUP)
        entries(start, SIB_GROUP, 512)
        entries(start, SIB_GROUP, 768)
        return carry

    def own_high(h, carry):
        entries(pl.multiple_of(h * 2 * GROUP, 2 * GROUP), 2 * GROUP, 256)
        return carry

    def own_low(h, carry):
        entries(pl.multiple_of(h * 2 * GROUP, 2 * GROUP), 2 * GROUP, 0)
        return carry

    def sib_part(vec, g):
        return jnp.dot(
            vec[:, g * GROUP : g * GROUP + SIB_GROUP],
            tiles[g * GROUP : g * GROUP + SIB_GROUP, 512:],
            preferred_element_type=F32,
        )

    def pieces(ref, values, first):
        for k in range(values.shape[1] // PIECE):
            ref[first + k] = values[:, k * PIECE : (k + 1) * PIECE]

    def spread(sib_got, out, got, which, order):
        copies = []
        for k in order:
            out[k] = out[k] + sib_got[k]
            copies.append(
                remote(out.at[k], got.at[k], rs_send.at[4 * which + k], rs_recv.at[4 * which + k], sum_to[k])
            )
            copies[-1].start()
        return copies

    def collect(copies, sib_got, out, got):
        mine = out[0] + sib_got[0]
        for copy in copies:
            copy.wait_recv()
        return mine + got[1] + got[2] + got[3]

    swap1 = remote(sib1, sib_got1, sib_send.at[0], sib_recv.at[0], sibling)
    swap2 = remote(sib2, sib_got2, sib_send.at[1], sib_recv.at[1], sibling)

    lax.fori_loop(0, 4, sib_group, 0)
    for copy in v1_copies:
        copy.wait_recv()
    lay_out(v1, v1_slots, 0, 16)
    pieces(sib1, sib_part(v1, 0) + sib_part(v1, 1) + sib_part(v1, 2) + sib_part(v1, 3), 0)
    swap1.start()
    lax.fori_loop(0, 2, own_high, 0)
    pieces(out1, jnp.dot(v1[...], tiles[:, 256:512], preferred_element_type=F32), 2)
    swap1.wait_recv()
    sums1 = spread(sib_got1, out1, got1, 0, (2, 3))
    lax.fori_loop(0, 2, own_low, 0)
    pieces(out1, jnp.dot(v1[...], tiles[:, :256], preferred_element_type=F32), 0)
    sums1 = sums1 + spread(sib_got1, out1, got1, 0, (1,))
    right = right_v[...]
    nugget = jnp.broadcast_to(nugget_v[...], (NRHS, PIECE))
    image = nugget * right + AMP * collect(sums1, sib_got1, out1, got1)
    step_to = right - STEP * image
    rounded = step_to.astype(BF16)
    v2_slots[0] = rounded
    p_rows[0] = rounded
    v2_copies = [
        remote(v2_slots.at[0], v2_slots.at[i], v2_send.at[i], v2_recv.at[i], col_to[i]) for i in FAR_FIRST
    ]
    pr_copies = [
        remote(v2_slots.at[0], p_rows.at[k], pr_send.at[k], pr_recv.at[k], row_to[k]) for k in (2, 1, 3)
    ]
    for copy in pr_copies + v2_copies:
        copy.start()
    hand_on = remote(
        p_rows.at[pl.ds(0, 4)], p_rows.at[pl.ds(4, 4)],
        pr_send.at[4], pr_recv.at[4], sibling,
    )

    ones = jnp.ones((8, PIECE), F32)

    def across(values):
        return lax.dot_general(
            ones, values, (((1,), (1,)), ((), ())), precision=lax.Precision.HIGHEST, preferred_element_type=F32
        )

    sums_a = across(jnp.concatenate([right * right, right * image], axis=0))
    ar[0, 0:1, :] = sums_a[0:1]

    mixed = jnp.zeros((NRHS, 4 * PIECE), F32)
    total = jnp.zeros((NRHS, 4 * PIECE), F32)
    for g in range(4):
        for copy, i in zip(v2_copies, FAR_FIRST):
            if i // 4 == g:
                copy.wait_recv()
        lay_out(v2, v2_slots, 4 * g, 4 * g + 4)
        mixed = mixed + sib_part(v2, g)
        if g == 3:
            for copy in pr_copies:
                copy.wait_recv()
            hand_on.start()
        total = total + jnp.dot(
            v2[:, g * GROUP : (g + 1) * GROUP],
            tiles[g * GROUP : (g + 1) * GROUP, :512],
            preferred_element_type=F32,
        )
    pieces(sib2, mixed, 0)
    pieces(out2, total, 0)
    form = jnp.zeros((NRHS, PIECE), F32)
    for k in range(4):
        form = form + p_rows[k].astype(F32) * out2[k]
    hand_on.wait_recv()
    for k in range(4):
        form = form + p_rows[k + 4].astype(F32) * sib2[k]
    form = nugget * step_to * step_to + AMP * form
    sums_b = across(jnp.concatenate([step_to * step_to, form], axis=0))
    ar[0, 1:2, :] = sums_b[0:1]

    def share(base, line):
        copies = [
            remote(
                ar.at[base], ar.at[base + k], ar_send.at[base + k], ar_recv.at[base + k], line[k],
            )
            for k in range(1, len(line))
        ]
        for copy in copies:
            copy.start()
        return copies

    def gathered(base, copies):
        for copy in copies:
            copy.wait_recv()
        terms = [ar[base + k] for k in range(len(copies) + 1)]
        while len(terms) > 1:
            terms = [a + b for a, b in zip(terms[::2], terms[1::2])]
        return terms[0]

    shares_y = share(0, y_line)
    swap2.start()
    swap2.wait_recv()
    sums2 = spread(sib_got2, out2, got2, 1, (2, 1, 3))
    ar[16] = gathered(0, shares_y)
    shares_plane = share(16, plane_line)
    second_image = nugget * step_to + AMP * collect(sums2, sib_got2, out2, got2)
    total = gathered(16, shares_plane)

    top, low = total[0:1], total[1:2]
    rr, ru = top, pltpu.roll(top, 64, 1)
    pp, pw = low, pltpu.roll(low, 64, 1)
    alpha = rr / ru
    share_p = alpha / STEP
    share_r = 1.0 - share_p
    rp = rr - STEP * ru
    pu = (rp - pp) / STEP
    rr_next = share_r * share_r * rr + 2.0 * share_r * share_p * rp + share_p * share_p * pp
    dir_r = share_r + rr_next / rr
    bend = dir_r * dir_r * ru + 2.0 * dir_r * share_p * pu + share_p * share_p * pw
    alpha_next = rr_next / bend
    along = alpha_next * dir_r
    coefs = jnp.concatenate(
        [
            alpha + along,
            alpha_next * share_p,
            share_r - along / STEP,
            share_p + along / STEP,
            -alpha_next * share_p,
            jnp.zeros((3, PIECE), F32),
        ],
        axis=0,
    )
    columns = coefs.T[:NRHS]
    out_ref[:NRHS] = columns[:, 0:1] * right + columns[:, 1:2] * step_to
    out_ref[NRHS:] = columns[:, 2:3] * right + columns[:, 3:4] * step_to + columns[:, 4:5] * second_image

    for copy in (
        row_copies + col_copies + v1_copies + sums1 + v2_copies + pr_copies + sums2
        + [swap1, swap2, hand_on] + shares_y + shares_plane
    ):
        copy.wait_send()


def on_device(points, right_side, nugget, scales, pairs):
    dma = pltpu.SemaphoreType.DMA
    operands = (points, right_side, nugget.reshape(1, PIECE), scales, pairs.T)
    operands = [pltpu.with_memory_space_constraint(array, pltpu.HBM) for array in operands]
    far_space = pl.BlockSpec(memory_space=pltpu.HBM)
    both = pl.pallas_call(
        kernel,
        out_shape=jax.ShapeDtypeStruct((2 * NRHS, PIECE), F32),
        in_specs=[far_space] * 5,
        out_specs=pl.BlockSpec(memory_space=pltpu.VMEM),
        scratch_shapes=[
            pltpu.VMEM((16, FEAT, PIECE), BF16),
            pltpu.VMEM((8, FEAT, PIECE), BF16),
            pltpu.VMEM((NRHS, PIECE), F32),
            pltpu.VMEM((1, PIECE), F32),
            pltpu.SMEM((FEAT,), F32),
            pltpu.SMEM((3, 32), jnp.int32),
            pltpu.SMEM((8,), F32),
            pltpu.VMEM((FEAT, PIECE), F32),
            pltpu.VMEM((4 * FEAT, 8 * PIECE), BF16),
            pltpu.VMEM((4 * FEAT, 16 * PIECE), BF16),
            pltpu.VMEM((16 * PIECE, 8 * PIECE), BF16),
            pltpu.VMEM((NRHS, 16 * PIECE), BF16),
            pltpu.VMEM((NRHS, 16 * PIECE), BF16),
            pltpu.VMEM((16, NRHS, PIECE), BF16),
            pltpu.VMEM((16, NRHS, PIECE), BF16),
            pltpu.VMEM((8, NRHS, PIECE), BF16),
        ]
        + [pltpu.VMEM((4, NRHS, PIECE), F32)] * 8
        + [
            pltpu.VMEM((48, 2, PIECE), F32),
            dma((5,)),
            dma((16,)), dma((16,)), dma((8,)), dma((8,)),
            dma((16,)), dma((16,)), dma((16,)), dma((16,)),
            dma((8,)), dma((8,)),
            dma((2,)), dma((2,)), dma((8,)), dma((8,)), dma((48,)), dma((48,)),
        ],
        compiler_params=pltpu.CompilerParams(
            collective_id=0, has_side_effects=True, vmem_limit_bytes=40 * 2**20
        ),
    )(*operands)
    return both[:NRHS], both[NRHS:]


def solution(mesh):
    placed = (P(None, ("blk", "grp")), P(None, ("blk", "grp")), P(("blk", "grp")), P(), P())
    return jax.shard_map(
        on_device,
        mesh=mesh,
        in_specs=placed,
        out_specs=(P(None, ("blk", "grp")), P(None, ("blk", "grp"))),
        check_vma=False,
    )
```

```python
import jax
import jax.numpy as jnp
from jax import lax
from jax.experimental import pallas as pl
from jax.experimental.pallas import tpu as pltpu
from jax.sharding import PartitionSpec as P

MESH = pl.DeviceIdType.MESH
F32 = jnp.float32
BF16 = jnp.bfloat16
STEP = 0.38
FAR = 64.0
PIECE = 128
NRHS = 64
FEAT = 16
AMP = 1.0 / 2064.0 / 256.0
SHIFTS = (0, 1, 3, 2)
GROUP = 4 * PIECE
SIB_GROUP = 3 * PIECE
FAR_FIRST = [4 * g + j for g in (3, 2, 1, 0) for j in (2, 1, 3, 0)][:-1]


def split3(value):
    first = value.astype(BF16).astype(F32)
    rest = value - first
    second = rest.astype(BF16).astype(F32)
    return first, second, rest - second


def kernel(
    points_ref, right_ref, nugget_ref, scales_ref, pairs_ref,
    out_ref,
    col_pts, row_pts, right_v, nugget_v, scales_s, pairs_s, pen_s,
    inv_v, row_ops, col_ops, tiles,
    v1, v2, v1_slots, v2_slots, p_rows, out1, out2, sib1, sib2, got1, got2, sib_got1, sib_got2, ar,
    local_sem, pts_send, pts_recv, rpts_send, rpts_recv, v1_send, v1_recv, v2_send, v2_recv,
    pr_send, pr_recv, sib_send, sib_recv, rs_send, rs_recv, ar_send, ar_recv,
):
    blk, grp = lax.axis_index("blk"), lax.axis_index("grp")
    chip, core = blk // 2, blk % 2
    side = 1 - 2 * core
    zlow = chip % 2
    zhigh, xat = grp // 4, grp % 4

    def device(chip_at, core_at, zhigh_at, x_at):
        return (
            lax.rem(chip_at + 32, 16) * 2 + core_at,
            lax.rem(zhigh_at + 8, 4) * 4 + lax.rem(x_at + 8, 4),
        )

    col_to = [
        device(chip + dm, cc, zhigh, xat + dx)
        for dx in SHIFTS
        for dm, cc in ((0, core), (side, core), (-side, 1 - core), (-2 * side, 1 - core))
    ]
    col_from = [
        device(chip - dm, cc, zhigh, xat - dx)
        for dx in SHIFTS
        for dm, cc in ((0, core), (side, core), (side, 1 - core), (2 * side, 1 - core))
    ]
    row_to = [device(chip, cc, zhigh + k, xat) for cc in (core, 1 - core) for k in range(4)]
    sum_to = [device(chip, core, zhigh - k, xat) for k in range(4)]
    sibling = device(chip, 1 - core, zhigh, xat)
    y_line = [
        device(chip + 2 * k, cc, zhigh, xat)
        for cc, k in [(core, 0)] + [(cc, k) for k in (4, 3, 5, 2, 6, 1, 7, 0) for cc in (1 - core, core)][:-1]
    ]
    plane = sorted(
        ((min(2 * dz, 8 - 2 * dz) + (low if dz < 3 else -low) + min(dx, 4 - dx), dz, low, dx)
         for dz in range(4) for low in range(2) for dx in range(4)),
        key=lambda place: -place[0],
    )
    plane = plane[-1:] + plane[:-1]
    plane_line = [
        device(chip + low * (1 - 2 * zlow), core, zhigh + dz, xat + dx) for _, dz, low, dx in plane
    ]

    far_y = [device(chip + 8, cc, zhigh, xat) for cc in (core, 1 - core)]
    greet = [col_from[i] for i in FAR_FIRST] + [row_to[k] for k in (2, 6, 1, 3, 5, 7, 4)] + far_y
    barrier = pltpu.get_barrier_semaphore()
    for target in greet:
        pl.semaphore_signal(barrier, inc=1, device_id=target, device_id_type=MESH)

    loads = [
        pltpu.make_async_copy(points_ref, col_pts.at[0], local_sem.at[0]),
        pltpu.make_async_copy(right_ref, right_v, local_sem.at[1]),
        pltpu.make_async_copy(scales_ref, scales_s, local_sem.at[2]),
        pltpu.make_async_copy(pairs_ref, pairs_s, local_sem.at[3]),
        pltpu.make_async_copy(nugget_ref, nugget_v, local_sem.at[4]),
    ]
    for load in loads:
        load.start()

    def remote(src, dst, send, recv, target):
        return pltpu.make_async_remote_copy(
            src_ref=src, dst_ref=dst, send_sem=send, recv_sem=recv, device_id=target, device_id_type=MESH
        )

    def lay_out(vec, slots, first, last):
        for i in range(first, last):
            vec[:, i * PIECE : (i + 1) * PIECE] = slots[i]

    loads[0].wait()
    pl.semaphore_wait(barrier, len(greet))
    row_copies = [
        remote(col_pts.at[0], row_pts.at[k], rpts_send.at[k], rpts_recv.at[k], row_to[k])
        for k in (2, 6, 1, 3, 5, 7, 4)
    ]
    col_copies = [
        remote(col_pts.at[0], col_pts.at[i], pts_send.at[i], pts_recv.at[i], col_to[i]) for i in FAR_FIRST
    ]
    for copy in row_copies + col_copies:
        copy.start()
    row_pts[0] = col_pts[0]

    loads[1].wait()
    v1_slots[0] = right_v[...].astype(BF16)
    v1_copies = [
        remote(v1_slots.at[0], v1_slots.at[i], v1_send.at[i], v1_recv.at[i], col_to[i]) for i in FAR_FIRST
    ]
    for copy in v1_copies:
        copy.start()

    for load in loads[2:]:
        load.wait()
    for f in range(FEAT):
        inv_v[f : f + 1, :] = jnp.full((1, PIECE), scales_s[f], F32)
    inv_v[...] = 1.0 / (inv_v[...] * inv_v[...])

    def away(low, offset):
        value = pairs_s[offset - 1, lax.rem(low + 32, 32)]
        return (1 - value).astype(F32) * FAR

    first = core == 0
    pen_s[0] = 0.0
    pen_s[1] = away(jnp.where(first, blk - 2, blk), 2)
    pen_s[2] = away(jnp.where(first, blk - 1, blk), 1)
    pen_s[3] = away(jnp.where(first, blk - 3, blk), 3)
    pen_s[4] = away(jnp.where(first, blk, blk - 1), 1)
    pen_s[5] = away(jnp.where(first, blk - 2, blk - 1), 3)
    pen_s[6] = away(jnp.where(first, blk - 1, blk - 1), 2)
    pen_s[7] = FAR

    at_row = lax.broadcasted_iota(jnp.int32, (FEAT, PIECE), 0)

    def norm_rows(pts):
        norm = jnp.sum(pts * pts * (16.0 * inv_v[...]), axis=0, keepdims=True)
        return [jnp.broadcast_to(part, (FEAT, PIECE)) for part in split3(norm)]

    for k in range(8):
        if k:
            remote(col_pts.at[0], row_pts.at[k], rpts_send.at[k], rpts_recv.at[k], sibling).wait_recv()
        pts = row_pts[k].astype(F32)
        one, two, three = norm_rows(pts)
        own = at_row == (6 if k < 4 else 7)
        extra = jnp.where((at_row < 3) | own, 1.0, 0.0)
        extra = jnp.where(at_row == 3, one, extra)
        extra = jnp.where(at_row == 4, two, extra)
        extra = jnp.where(at_row == 5, three, extra)
        span = slice(k * PIECE, (k + 1) * PIECE)
        for part in range(3):
            row_ops[part * FEAT : (part + 1) * FEAT, span] = row_pts[k]
        row_ops[3 * FEAT :, span] = extra.astype(BF16)

    def prepare(g):
        for j in range(4):
            i = g * 4 + j

            def arrived():
                remote(col_pts.at[0], col_pts.at[i], pts_send.at[i], pts_recv.at[i], sibling).wait_recv()

            if j == 0:
                pl.when(i > 0)(arrived)
            else:
                arrived()
            pts = col_pts[i].astype(F32)
            scaled = split3(pts * (-32.0 * inv_v[...]))
            one, two, three = norm_rows(pts)
            extra = jnp.where(at_row == 0, one, 0.0)
            extra = jnp.where(at_row == 1, two, extra)
            extra = jnp.where(at_row == 2, three, extra)
            extra = jnp.where((at_row >= 3) & (at_row < 6), 1.0, extra)
            extra = jnp.where(at_row == 6, pen_s[j], extra)
            extra = jnp.where(at_row == 7, pen_s[j + 4], extra)
            at = pl.ds(pl.multiple_of(i * PIECE, PIECE), PIECE)
            for part in range(3):
                col_ops[part * FEAT : (part + 1) * FEAT, at] = scaled[part].astype(BF16)
            col_ops[3 * FEAT :, at] = extra.astype(BF16)

    def entries(start, depth, first_row):
        at = pl.ds(start, depth)
        span = slice(first_row, first_row + 256)
        squared = lax.dot_general(
            col_ops[:, at], row_ops[:, span], (((0,), (0,)), ((), ())), preferred_element_type=F32
        )
        squared = jnp.maximum(squared, 1e-12)
        spare = jnp.maximum(4.0 - squared * lax.rsqrt(squared), 0.0)
        second = spare * spare
        tiles[at, span] = (second * second * (5.0 - spare)).astype(BF16)

    def sib_group(g, carry):
        prepare(g)
        start = pl.multiple_of(g * GROUP, GROUP)
        entries(start, SIB_GROUP, 512)
        entries(start, SIB_GROUP, 768)
        return carry

    def own_high(h, carry):
        entries(pl.multiple_of(h * 2 * GROUP, 2 * GROUP), 2 * GROUP, 256)
        return carry

    def own_low(h, carry):
        entries(pl.multiple_of(h * 2 * GROUP, 2 * GROUP), 2 * GROUP, 0)
        return carry

    def sib_part(vec, g):
        return jnp.dot(
            vec[:, g * GROUP : g * GROUP + SIB_GROUP],
            tiles[g * GROUP : g * GROUP + SIB_GROUP, 512:],
            preferred_element_type=F32,
        )

    def pieces(ref, values, first):
        for k in range(values.shape[1] // PIECE):
            ref[first + k] = values[:, k * PIECE : (k + 1) * PIECE]

    def spread(sib_got, out, got, which, order):
        copies = []
        for k in order:
            out[k] = out[k] + sib_got[k]
            copies.append(
                remote(out.at[k], got.at[k], rs_send.at[4 * which + k], rs_recv.at[4 * which + k], sum_to[k])
            )
            copies[-1].start()
        return copies

    def collect(copies, sib_got, out, got):
        mine = out[0] + sib_got[0]
        for copy in copies:
            copy.wait_recv()
        return mine + got[1] + got[2] + got[3]

    swap1 = remote(sib1, sib_got1, sib_send.at[0], sib_recv.at[0], sibling)
    swap2 = remote(sib2, sib_got2, sib_send.at[1], sib_recv.at[1], sibling)

    lax.fori_loop(0, 4, sib_group, 0)
    for copy in v1_copies:
        copy.wait_recv()
    lay_out(v1, v1_slots, 0, 16)
    pieces(sib1, sib_part(v1, 0) + sib_part(v1, 1) + sib_part(v1, 2) + sib_part(v1, 3), 0)
    swap1.start()
    lax.fori_loop(0, 2, own_high, 0)
    pieces(out1, jnp.dot(v1[...], tiles[:, 256:512], preferred_element_type=F32), 2)
    swap1.wait_recv()
    sums1 = spread(sib_got1, out1, got1, 0, (2, 3))
    lax.fori_loop(0, 2, own_low, 0)
    pieces(out1, jnp.dot(v1[...], tiles[:, :256], preferred_element_type=F32), 0)
    sums1 = sums1 + spread(sib_got1, out1, got1, 0, (1,))
    right = right_v[...]
    nugget = jnp.broadcast_to(nugget_v[...], (NRHS, PIECE))
    image = nugget * right + AMP * collect(sums1, sib_got1, out1, got1)
    step_to = right - STEP * image
    rounded = step_to.astype(BF16)
    v2_slots[0] = rounded
    p_rows[0] = rounded
    v2_copies = [
        remote(v2_slots.at[0], v2_slots.at[i], v2_send.at[i], v2_recv.at[i], col_to[i]) for i in FAR_FIRST
    ]
    across_z, next_z, twin = (
        remote(v2_slots.at[0], p_rows.at[k], pr_send.at[k], pr_recv.at[k], target)
        for k, target in ((2, row_to[2]), (3, row_to[1]), (4, sibling))
    )
    upper = zhigh >= 2

    @pl.when(upper)
    def _():
        across_z.start()
        p_rows[2] = jnp.zeros((NRHS, PIECE), BF16)

    for copy in [next_z] + v2_copies + [twin]:
        copy.start()
    hand_on = remote(
        p_rows.at[pl.ds(2, 2)], p_rows.at[pl.ds(6, 2)], pr_send.at[5], pr_recv.at[5], sibling
    )

    ones = jnp.ones((8, PIECE), F32)

    def across(values):
        return lax.dot_general(
            ones, values, (((1,), (1,)), ((), ())), precision=lax.Precision.HIGHEST, preferred_element_type=F32
        )

    sums_a = across(jnp.concatenate([right * right, right * image], axis=0))
    ar[0, 0:1, :] = sums_a[0:1]

    mixed = jnp.zeros((NRHS, 4 * PIECE), F32)
    total = jnp.zeros((NRHS, 4 * PIECE), F32)
    for g in range(4):
        for copy, i in zip(v2_copies, FAR_FIRST):
            if i // 4 == g:
                copy.wait_recv()
        lay_out(v2, v2_slots, 4 * g, 4 * g + 4)
        mixed = mixed + sib_part(v2, g)
        if g == 3:
            next_z.wait_recv()
            pl.when(zhigh < 2)(across_z.wait_recv)
            hand_on.start()
        total = total + jnp.dot(
            v2[:, g * GROUP : (g + 1) * GROUP],
            tiles[g * GROUP : (g + 1) * GROUP, :512],
            preferred_element_type=F32,
        )
    pieces(sib2, mixed, 0)
    pieces(out2, total, 0)
    form = 2.0 * (p_rows[2].astype(F32) * out2[2] + p_rows[3].astype(F32) * out2[1])
    form = form + p_rows[0].astype(F32) * out2[0]
    twin.wait_recv()
    form = form + p_rows[4].astype(F32) * sib2[0]
    hand_on.wait_recv()
    form = form + 2.0 * (p_rows[6].astype(F32) * sib2[2] + p_rows[7].astype(F32) * sib2[1])
    form = nugget * step_to * step_to + AMP * form
    sums_b = across(jnp.concatenate([step_to * step_to, form], axis=0))
    ar[0, 1:2, :] = sums_b[0:1]

    def share(base, line):
        copies = [
            remote(
                ar.at[base], ar.at[base + k], ar_send.at[base + k], ar_recv.at[base + k], line[k],
            )
            for k in range(1, len(line))
        ]
        for copy in copies:
            copy.start()
        return copies

    def gathered(base, copies):
        for copy in copies:
            copy.wait_recv()
        terms = [ar[base + k] for k in range(len(copies) + 1)]
        while len(terms) > 1:
            terms = [a + b for a, b in zip(terms[::2], terms[1::2])]
        return terms[0]

    shares_y = share(0, y_line)
    swap2.start()
    swap2.wait_recv()
    sums2 = spread(sib_got2, out2, got2, 1, (2, 1, 3))
    ar[16] = gathered(0, shares_y)
    shares_plane = share(16, plane_line)
    second_image = nugget * step_to + AMP * collect(sums2, sib_got2, out2, got2)
    total = gathered(16, shares_plane)

    top, low = total[0:1], total[1:2]
    rr, ru = top, pltpu.roll(top, 64, 1)
    pp, pw = low, pltpu.roll(low, 64, 1)
    alpha = rr / ru
    share_p = alpha / STEP
    share_r = 1.0 - share_p
    rp = rr - STEP * ru
    pu = (rp - pp) / STEP
    rr_next = share_r * share_r * rr + 2.0 * share_r * share_p * rp + share_p * share_p * pp
    dir_r = share_r + rr_next / rr
    bend = dir_r * dir_r * ru + 2.0 * dir_r * share_p * pu + share_p * share_p * pw
    alpha_next = rr_next / bend
    along = alpha_next * dir_r
    coefs = jnp.concatenate(
        [
            alpha + along,
            alpha_next * share_p,
            share_r - along / STEP,
            share_p + along / STEP,
            -alpha_next * share_p,
            jnp.zeros((3, PIECE), F32),
        ],
        axis=0,
    )
    columns = coefs.T[:NRHS]
    out_ref[:NRHS] = columns[:, 0:1] * right + columns[:, 1:2] * step_to
    out_ref[NRHS:] = columns[:, 2:3] * right + columns[:, 3:4] * step_to + columns[:, 4:5] * second_image

    for copy in (
        row_copies + col_copies + v1_copies + sums1 + v2_copies + [next_z, twin] + sums2
        + [swap1, swap2, hand_on] + shares_y + shares_plane
    ):
        copy.wait_send()
    pl.when(upper)(across_z.wait_send)


def on_device(points, right_side, nugget, scales, pairs):
    dma = pltpu.SemaphoreType.DMA
    operands = (points, right_side, nugget.reshape(1, PIECE), scales, pairs.T)
    operands = [pltpu.with_memory_space_constraint(array, pltpu.HBM) for array in operands]
    far_space = pl.BlockSpec(memory_space=pltpu.HBM)
    both = pl.pallas_call(
        kernel,
        out_shape=jax.ShapeDtypeStruct((2 * NRHS, PIECE), F32),
        in_specs=[far_space] * 5,
        out_specs=pl.BlockSpec(memory_space=pltpu.VMEM),
        scratch_shapes=[
            pltpu.VMEM((16, FEAT, PIECE), BF16),
            pltpu.VMEM((8, FEAT, PIECE), BF16),
            pltpu.VMEM((NRHS, PIECE), F32),
            pltpu.VMEM((1, PIECE), F32),
            pltpu.SMEM((FEAT,), F32),
            pltpu.SMEM((3, 32), jnp.int32),
            pltpu.SMEM((8,), F32),
            pltpu.VMEM((FEAT, PIECE), F32),
            pltpu.VMEM((4 * FEAT, 8 * PIECE), BF16),
            pltpu.VMEM((4 * FEAT, 16 * PIECE), BF16),
            pltpu.VMEM((16 * PIECE, 8 * PIECE), BF16),
            pltpu.VMEM((NRHS, 16 * PIECE), BF16),
            pltpu.VMEM((NRHS, 16 * PIECE), BF16),
            pltpu.VMEM((16, NRHS, PIECE), BF16),
            pltpu.VMEM((16, NRHS, PIECE), BF16),
            pltpu.VMEM((8, NRHS, PIECE), BF16),
        ]
        + [pltpu.VMEM((4, NRHS, PIECE), F32)] * 8
        + [
            pltpu.VMEM((48, 2, PIECE), F32),
            dma((5,)),
            dma((16,)), dma((16,)), dma((8,)), dma((8,)),
            dma((16,)), dma((16,)), dma((16,)), dma((16,)),
            dma((8,)), dma((8,)),
            dma((2,)), dma((2,)), dma((8,)), dma((8,)), dma((48,)), dma((48,)),
        ],
        compiler_params=pltpu.CompilerParams(
            collective_id=0, has_side_effects=True, vmem_limit_bytes=40 * 2**20
        ),
    )(*operands)
    return both[:NRHS], both[NRHS:]


def solution(mesh):
    placed = (P(None, ("blk", "grp")), P(None, ("blk", "grp")), P(("blk", "grp")), P(), P())
    return jax.shard_map(
        on_device,
        mesh=mesh,
        in_specs=placed,
        out_specs=(P(None, ("blk", "grp")), P(None, ("blk", "grp"))),
        check_vma=False,
    )
```
